128 devices in a mesh: group: 8 (over y, core), blk: 16 (over x, z).
Axes of the slice: x: 4, y: 4, z: 4, core: 2. Of those that a mesh axis runs over, the one named last changes fastest.
Arguments:
- gradient: bfloat16 [128, 512, 2304], P(None, ('group', 'blk')), may hold values from -60 to 60
- momentum: float32 [128, 512, 2304], P(None, ('group', 'blk')), may hold values from -3 to 3
- owner_group: int32 [128, 1], replicated, may hold values from 0 to 7; in each aligned block of 128 rows (0 to 127, 128 to 255, ...) at most 32 rows name the same one
Outputs:
- update: bfloat16 [128, 512, 2304], P(None, ('group', 'blk'))
- momentum_out: float32 [128, 512, 2304], P(None, ('group', 'blk'))
- slot_rms: float32 [8, 32], P('group', 'blk')
The draws below stay inside these ranges and needn't reach their ends.
Inputs may be any that keep to these rules, and one draw needn't show every extreme that they name: `owner_group`: each group is named by at most 32 matrices, and one group by exactly that many.
All inputs are finite; a program needn't handle non-finite values.
Results may differ from the reference program's by a relative error of at most 0.02.
Values may be sent and summed in bfloat16 or wider, within the bound.
A program may use at most 128 MiB of HBM per device.

```python
import math
import jax
import jax.numpy as jnp
import numpy as np
from jax import lax

D = 2304
H = 512
ITERS = 5
SLOTS = 2
M = 128
N_GROUP = 8
N_BLK = 16


def draw_gradient(key, part):
    key = jax.random.fold_in(key, 11)
    key_noise, key_jitter, key_column = jax.random.split(key, 3)
    rising = 0.95 * jnp.arange(H, dtype=jnp.float32) / H
    jitter = jax.random.uniform(key_jitter, (M, H, 1), jnp.float32, -0.05, 0.05)
    row_scale = 10.0 ** (rising[None, :, None] + jitter)
    column_scale = 10.0 ** jax.random.uniform(key_column, (M, 1, D), jnp.float32, 0.0, 1.0)
    values = 0.1 * jnp.clip(jax.random.normal(key_noise, (M, H, D), jnp.float32), -6.0, 6.0)
    return (values * row_scale * column_scale).astype(jnp.bfloat16)


def levels(stream_key, dims, cuts, smallest, largest):
    loudness = 1.0
    for dim, blocks in cuts:
        heights = jax.random.uniform(jax.random.fold_in(jax.random.fold_in(stream_key, 6), dim), (blocks,), jnp.float32, smallest / len(cuts), largest / len(cuts))
        loudness = loudness * jnp.repeat(jnp.exp(heights), dims[dim] // blocks).reshape((-1,) + (1,) * (len(dims) - 1 - dim))
    return loudness


def deal_out(own_key, own, number, rows, number_of, top, reach, skew):
    sequence = jax.random.permutation(own_key, number_of)
    packed, usual = shares(number_of, rows * top, reach, skew, True), shares(number_of, rows * top, reach, skew, False)
    places = jnp.arange(number_of)

    def named(lengths, turn):
        used = int((lengths > 0).sum())
        fixed = max(1, used // 4)
        moved = fixed + (places - fixed + turn * (used - fixed)) % max(1, number_of - fixed)
        return jnp.zeros((number_of,), jnp.int32).at[sequence[jnp.where(places < fixed, places, moved)]].set(jnp.asarray(lengths, jnp.int32))

    lengths = jnp.where(number % 4 == 0, named(packed, number // 4), named(usual, number - number // 4 - 1))
    mixed = jax.random.permutation(jax.random.fold_in(own, 3), number_of)
    source_of, receiver = mixed[0:number_of // 2 * 2:2], mixed[1:number_of // 2 * 2:2]
    margin = jnp.minimum(lengths[source_of] - 1, reach - lengths[receiver]) // 2
    margin = jnp.where((source_of == sequence[0]) | (receiver == sequence[0]) | (lengths[receiver] == 0), 0, jnp.maximum(margin, 0))
    moved = jax.random.randint(jax.random.fold_in(own, 4), (number_of // 2,), 0, 1 << 20) % (margin + 1)
    lengths = lengths.at[source_of].add(-moved).at[receiver].add(moved)
    items = jnp.searchsorted(jnp.cumsum(lengths), jnp.arange(rows * top), side="right").astype(jnp.int32)
    grid = items.reshape(top, rows).T
    grid = grid[jax.random.permutation(jax.random.fold_in(own, 1), rows)]
    turn = jax.random.randint(jax.random.fold_in(own, 2), (rows, 1), 0, top)
    return jnp.take_along_axis(grid, (jnp.arange(top)[None, :] + turn) % top, axis=1)


def shares(count, total, reach, slope, full):
    loads = [(1 << 20) // math.isqrt(rank ** slope) + 1 for rank in range(1, count + 1)]
    largest = reach if full else min(reach, max(-(-total // count), total * loads[0] // sum(loads)))
    least = 1 if total - largest >= count - 1 else 0
    counts, rest = [largest] + [least] * (count - 1), total - largest - least * (count - 1)
    while rest > 0:
        free = [i for i in range(1, count) if counts[i] < largest] or [i for i in range(1, count) if counts[i] < reach]
        pool, budget = sum([loads[i] for i in free]), rest
        for i in free:
            addition = min(reach - counts[i], max(1, budget * loads[i] // pool), rest)
            counts[i] = counts[i] + addition
            rest = rest - addition
    return np.array(counts)


def bell_draw(own_key, shape, width, reach, cuts=(), kind=jnp.bfloat16):
    drawn = jax.random.normal(own_key, shape, jnp.float32) * width
    if len(cuts) > 0:
        drawn = levels(own_key, shape, cuts, -0.22, 0.18) * drawn
    return jnp.clip(drawn, min=-reach, max=reach).astype(kind)


def setup_inputs(seed: int = 0) -> dict:
    splits = jax.random.split(jax.random.key(seed), 4)
    gradient = draw_gradient(jax.random.fold_in(splits[3], 71), 0)
    momentum = bell_draw(splits[1], (M, H, D), 0.5, 3.0, ((1, 128),), jnp.float32)
    owner_group_keys = jax.random.split(jax.random.fold_in(splits[2], 1), M // M)
    owner_group_turns = jax.random.permutation(jax.random.fold_in(splits[2], 3), M // M)
    owner_group = jax.vmap(lambda own, number: deal_out(jax.random.fold_in(splits[2], 2), own, number, M, N_GROUP, 1, SLOTS * N_BLK, 2))(owner_group_keys, owner_group_turns).reshape((M, 1))
    return dict(gradient=gradient, momentum=momentum, owner_group=owner_group)


linear_coefficient = 3.4445
coef_b = -4.775
coef_c = 2.0315
decay_rate = 0.95
epsilon = 1e-06

def widen(value):
    return lax.optimization_barrier(value).astype(jnp.float32)

def product(left, right):
    return jnp.dot(left, right, preferred_element_type=jnp.float32, precision=lax.Precision.HIGHEST)

def orthogonalize(current):
    for repeat in range(ITERS):
        wide = widen(current)
        gram_product = product(wide, wide.T).astype(jnp.bfloat16)
        gram_wide = widen(gram_product)
        gram_squared = product(gram_wide, gram_wide)
        poly = (coef_b * gram_wide + coef_c * gram_squared).astype(jnp.bfloat16)
        current = (linear_coefficient * wide + product(widen(poly), wide)).astype(jnp.bfloat16)
    return current

def per_matrix(item):
    grad_one, momentum_one = item
    moved = decay_rate * momentum_one + grad_one.astype(jnp.float32)
    magnitude = jnp.sqrt(jnp.sum(moved * moved))
    starting_matrix = (moved / (magnitude + epsilon)).astype(jnp.bfloat16)
    final = orthogonalize(starting_matrix)
    scale_factor = 0.2 * math.sqrt(max(H, D))
    update_one = (scale_factor * final.astype(jnp.float32)).astype(jnp.bfloat16)
    return (update_one, moved, magnitude)

def reference(gradient, momentum, owner_group):
    update, momentum_out, magnitudes = lax.map(per_matrix, (gradient, momentum))
    owners = owner_group[:, 0].astype(jnp.int32)
    positions = jnp.arange(M, dtype=jnp.int32)
    earlier = (owners[:, None] == owners[None, :]) & (positions[None, :] < positions[:, None])
    ranking = lax.optimization_barrier(jnp.sum(earlier.astype(jnp.int32), axis=1)).astype(jnp.int32)
    placing = (owners * (SLOTS * N_BLK) + ranking).astype(jnp.int32)
    spread = magnitudes / math.sqrt(H * D)
    table = jnp.zeros((N_GROUP * SLOTS * N_BLK,), jnp.float32).at[placing].set(spread)
    slot_rms = table.reshape(N_GROUP, SLOTS * N_BLK)
    return (update, momentum_out, slot_rms)
```

```python
import functools
import math

import jax
import jax.numpy as jnp
from jax import lax
from jax.experimental import pallas as pl
from jax.experimental.pallas import tpu as pltpu
from jax.sharding import PartitionSpec as P

ITERS = 5
SLOTS = 2
linear_coefficient = 3.4445
coef_b = -4.775
coef_c = 2.0315
decay_rate = 0.95
epsilon = 1e-06

MESH = pl.DeviceIdType.MESH
F32 = jnp.float32
BF16 = jnp.bfloat16
LANES = 128
CHUNKS = 8


def hops(offset):
    return sum(min(step, 4 - step) for step in offset[:3])


def offsets_far_first():
    every = []
    for i in range(64):
        a, b, c = i % 4, (i // 4) % 4, i // 16
        for dcore in range(2):
            every.append((a, (a + b) % 4, (3 * a + c) % 4, (dcore + a) % 2))
    every.remove((0, 0, 0, 0))
    return sorted(every, key=hops, reverse=True)


SEND_ORDER = offsets_far_first()


def shifted(offset):
    group, blk = lax.axis_index("group"), lax.axis_index("blk")
    dx, dy, dz, dcore = offset
    y = lax.rem(group // 2 + dy, 4)
    core = lax.rem(lax.rem(group, 2) + dcore, 2)
    x = lax.rem(blk // 4 + dx, 4)
    z = lax.rem(lax.rem(blk, 4) + dz, 4)
    return (y * 2 + core, x * 4 + z)


def slot_of(offset):
    dx, dy, dz, dcore = offset
    return ((dx * 4 + dy) * 4 + dz) * 2 + dcore


def eye(size):
    rows = lax.broadcasted_iota(jnp.int32, (size, size), 0)
    return rows == lax.broadcasted_iota(jnp.int32, (size, size), 1)


def diagonals(matrix):
    size = matrix.shape[0]
    on = eye(LANES)
    columns, rows = [], []
    for i in range(0, size, LANES):
        block = jnp.where(on, matrix[i : i + LANES, i : i + LANES], 0.0)
        columns.append(jnp.sum(block, axis=1, keepdims=True))
        rows.append(jnp.sum(block, axis=0, keepdims=True))
    return jnp.concatenate(columns, 0), jnp.concatenate(rows, 1)


def parted(matrix):
    column, row = diagonals(matrix)
    off = jnp.where(eye(matrix.shape[0]), 0.0, matrix)
    return matrix, off, off.astype(BF16), column, row


def times(left, right):
    inner = jnp.dot(left[2], right[2], preferred_element_type=F32)
    return inner + left[3] * right[0] + left[1] * right[4]


def polynomial_chain(gram_ref, factor_ref, turn_ref):
    for step in range(ITERS):
        gram = parted(gram_ref[...])
        square = times(gram, gram)
        one = jnp.where(eye(square.shape[0]), linear_coefficient, 0.0)
        poly = parted(coef_b * gram[0] + coef_c * square + one)
        last = step == ITERS - 1
        if not last:
            turn_ref[...] = times(poly, gram)
        if step == 0:
            factor_ref[...] = poly[0]
        else:
            factor_ref[...] = times(poly, parted(factor_ref[...]))
        if not last:
            gram_ref[...] = times(poly, parted(turn_ref[...]))


def kernel(
    gradient,
    momentum,
    owners_ref,
    update,
    momentum_out,
    slot_ref,
    grad_v,
    mom_v,
    tx,
    rx,
    tx2,
    rx2,
    upd_v,
    norms,
    gram_ref,
    factor_ref,
    turn_ref,
    grad_sem,
    mom_sem,
    out_sem,
    upd_sem,
    send_sem,
    recv_sem,
    send2_sem,
    recv2_sem,
    own_sem,
    norm_send,
    norm_recv,
    near_sem,
):
    group, blk = lax.axis_index("group"), lax.axis_index("blk")
    me = group * 16 + blk
    count, rows, width = grad_v.shape
    tiles = width // LANES
    full_rows = rows * count
    per = count // CHUNKS

    def load(c):
        part = pl.ds(c * per, per)
        return (
            pltpu.make_async_copy(gradient.at[part], grad_v.at[part], grad_sem.at[c]),
            pltpu.make_async_copy(momentum.at[part], mom_v.at[part], mom_sem.at[c]),
        )

    def store(c):
        part = pl.ds(c * per, per)
        return pltpu.make_async_copy(mom_v.at[part], momentum_out.at[part], out_sem.at[c])

    for c in range(CHUNKS):
        for copy in load(c):
            copy.start()

    barrier = pltpu.get_barrier_semaphore()
    first = [(dx, 0, 0, dc) for dx in range(4) for dc in range(2) if (dx, dc) != (0, 0)]
    second = [(0, dy, dz, 0) for dy in range(4) for dz in range(4) if (dy, dz) != (0, 0)]
    for offset in first + second:
        pl.semaphore_signal(barrier, inc=1, device_id=shifted(offset), device_id_type=MESH)

    def ready(c):
        for copy in load(c):
            copy.wait()

        @pl.loop(0, per)
        def _(i):
            m = c * per + i
            for j in range(tiles):
                lanes = pl.ds(j * LANES, LANES)
                new = decay_rate * mom_v[m, :, lanes] + grad_v[m, :, lanes].astype(F32)
                mom_v[m, :, lanes] = new
                tx[m, j] = new.astype(BF16)

        store(c).start()

    for c in range(CHUNKS // 2):
        ready(c)
    pl.semaphore_wait(barrier, len(first) + len(second))
    for offset in second:
        pl.semaphore_signal(near_sem, inc=1, device_id=shifted(offset), device_id_type=MESH)
    for c in range(CHUNKS // 2, CHUNKS):
        ready(c)
    pl.semaphore_wait(near_sem, len(second))

    def send(offset):
        device = shifted(offset)
        at = slot_of(offset)
        return pltpu.make_async_remote_copy(
            src_ref=tx.at[device[0] * 16 + device[1]],
            dst_ref=rx.at[:, me],
            send_sem=send_sem.at[at],
            recv_sem=recv_sem.at[at],
            device_id=device,
            device_id_type=MESH,
        )

    own = pltpu.make_async_copy(tx.at[me], rx.at[:, me], own_sem.at[0])
    own.start()
    for offset in SEND_ORDER:
        send(offset).start()

    def digits(k):
        return (k // 32, (k // 8) % 4, (k // 2) % 4, k % 2)

    own.wait()

    @pl.loop(1, count)
    def _(k):
        send(digits(k)).wait()

    x_in = rx.reshape(tiles, full_rows, LANES)
    gram = None
    for j in range(0, tiles, 2):
        pair = jnp.concatenate([x_in[j], x_in[j + 1]], axis=1)
        term = lax.dot_general(pair, pair, (((1,), (1,)), ((), ())), preferred_element_type=F32)
        gram = term if gram is None else gram + term
    norm = jnp.sqrt(jnp.sum(diagonals(gram)[1]))
    norms[me] = jnp.full((1, LANES), norm, F32)

    def spread_blk(k):
        return pltpu.make_async_remote_copy(
            src_ref=norms.at[me],
            dst_ref=norms.at[me],
            send_sem=norm_send.at[k],
            recv_sem=norm_recv.at[k],
            device_id=(group, lax.rem(blk + k, 16)),
            device_id_type=MESH,
        )

    def spread_group(k):
        part = pl.ds(group * 16, 16)
        return pltpu.make_async_remote_copy(
            src_ref=norms.at[part],
            dst_ref=norms.at[part],
            send_sem=norm_send.at[16 + k],
            recv_sem=norm_recv.at[16 + k],
            device_id=(lax.rem(group + k, 8), blk),
            device_id_type=MESH,
        )

    @pl.loop(1, 16)
    def _(k):
        spread_blk(k).start()

    inverse = 1.0 / (jnp.full((1, 1), norm, F32) + epsilon)
    gram_ref[...] = gram * (inverse * inverse)
    polynomial_chain(gram_ref, factor_ref, turn_ref)

    @pl.loop(1, 16)
    def _(k):
        spread_blk(k).wait()

    @pl.loop(1, 8)
    def _(k):
        spread_group(k).start()

    factor = parted(factor_ref[...])
    scale = 0.2 * math.sqrt(max(full_rows, width))
    x_out = tx2.reshape(tiles, full_rows, LANES)
    for j in range(0, tiles, 2):
        pair = jnp.concatenate([x_in[j], x_in[j + 1]], axis=1)
        mixed = jnp.dot(factor[2], pair, preferred_element_type=F32)
        final = ((mixed + factor[3] * pair.astype(F32)) * inverse).astype(BF16)
        scaled = (scale * final.astype(F32)).astype(BF16)
        x_out[j] = scaled[:, :LANES]
        x_out[j + 1] = scaled[:, LANES:]

    def back(offset):
        device = shifted(offset)
        at = slot_of(offset)
        return pltpu.make_async_remote_copy(
            src_ref=tx2.at[:, device[0] * 16 + device[1]],
            dst_ref=rx2.at[me],
            send_sem=send2_sem.at[at],
            recv_sem=recv2_sem.at[at],
            device_id=device,
            device_id_type=MESH,
        )

    own2 = pltpu.make_async_copy(tx2.at[:, me], rx2.at[me], own_sem.at[1])
    own2.start()
    for offset in SEND_ORDER:
        back(offset).start()

    @pl.loop(1, 8)
    def _(k):
        spread_group(k).wait()

    owner = jnp.broadcast_to(owners_ref[...], (count, LANES))
    other = jnp.transpose(owner.astype(F32)).astype(jnp.int32)
    row = lax.broadcasted_iota(jnp.int32, (count, LANES), 0)
    lane = lax.broadcasted_iota(jnp.int32, (count, LANES), 1)
    earlier = jnp.where((owner == other) & (lane < row), 1.0, 0.0)
    rank = jnp.sum(earlier, axis=1, keepdims=True).astype(jnp.int32)
    placing = owner * (SLOTS * 16) + rank
    spread = norms[:, 0, :] * (1.0 / math.sqrt(full_rows * width))
    chosen = jnp.where(placing == me * SLOTS + lane, spread, 0.0)
    slot_ref[...] = jnp.sum(chosen, axis=0, keepdims=True)[:, :SLOTS]

    def arrived(m):
        for j in range(tiles):
            upd_v[m, :, pl.ds(j * LANES, LANES)] = rx2[m, j]

    own2.wait()
    arrived(me)

    @pl.loop(0, count - 1)
    def _(i):
        dx, dy, dz, dc = digits(count - 1 - i)
        back((dx, dy, dz, dc)).wait()
        gone = shifted(((4 - dx) % 4, (4 - dy) % 4, (4 - dz) % 4, dc))
        arrived(gone[0] * 16 + gone[1])

    done = pltpu.make_async_copy(upd_v, update, upd_sem.at[0])
    done.start()
    for c in range(CHUNKS):
        store(c).wait()
    done.wait()


def on_device(gradient, momentum, owner_group):
    count, rows, width = gradient.shape
    tiles = width // LANES
    full_rows = rows * count
    wide = (count, tiles, rows, LANES)
    tall = (tiles, count, rows, LANES)
    square = pltpu.VMEM((full_rows, full_rows), F32)
    dma = pltpu.SemaphoreType.DMA
    return pl.pallas_call(
        kernel,
        out_shape=(
            jax.ShapeDtypeStruct(gradient.shape, BF16),
            jax.ShapeDtypeStruct(momentum.shape, F32),
            jax.ShapeDtypeStruct((1, SLOTS), F32),
        ),
        in_specs=[
            pl.BlockSpec(memory_space=pl.ANY),
            pl.BlockSpec(memory_space=pl.ANY),
            pl.BlockSpec(memory_space=pltpu.VMEM),
        ],
        out_specs=(
            pl.BlockSpec(memory_space=pl.ANY),
            pl.BlockSpec(memory_space=pl.ANY),
            pl.BlockSpec(memory_space=pltpu.VMEM),
        ),
        scratch_shapes=[
            pltpu.VMEM(gradient.shape, BF16),
            pltpu.VMEM(momentum.shape, F32),
            pltpu.VMEM(wide, BF16),
            pltpu.VMEM(tall, BF16),
            pltpu.VMEM(tall, BF16),
            pltpu.VMEM(wide, BF16),
            pltpu.VMEM(gradient.shape, BF16),
            pltpu.VMEM((count, 1, LANES), F32),
            square,
            square,
            square,
            dma((CHUNKS,)),
            dma((CHUNKS,)),
            dma((CHUNKS,)),
            dma((1,)),
            dma((count,)),
            dma((count,)),
            dma((count,)),
            dma((count,)),
            dma((2,)),
            dma((24,)),
            dma((24,)),
            pltpu.SemaphoreType.REGULAR,
        ],
        compiler_params=pltpu.CompilerParams(
            collective_id=0, has_side_effects=True, vmem_limit_bytes=50 << 20
        ),
    )(gradient, momentum, owner_group)


def solution(mesh):
    placed = (P(None, ("group", "blk"), None), P(None, ("group", "blk"), None), P())
    return jax.shard_map(
        on_device,
        mesh=mesh,
        in_specs=placed,
        out_specs=(
            P(None, ("group", "blk"), None),
            P(None, ("group", "blk"), None),
            P("group", "blk"),
        ),
        check_vma=False,
    )
```

```python
import functools
import math

import jax
import jax.numpy as jnp
from jax import lax
from jax.experimental import pallas as pl
from jax.experimental.pallas import tpu as pltpu
from jax.sharding import PartitionSpec as P

ITERS = 5
SLOTS = 2
linear_coefficient = 3.4445
coef_b = -4.775
coef_c = 2.0315
decay_rate = 0.95
epsilon = 1e-06

MESH = pl.DeviceIdType.MESH
F32 = jnp.float32
BF16 = jnp.bfloat16
LANES = 128
CHUNKS = 4


def hops(offset):
    return sum(min(step, 4 - step) for step in offset)


def chips_far_first():
    every = []
    for i in range(1, 64):
        a, b, c = i % 4, (i // 4) % 4, i // 16
        every.append((a, (a + b) % 4, (3 * a + c) % 4))
    return sorted(every, key=hops, reverse=True)


CHIP_ORDER = chips_far_first()


def shifted(offset):
    group, blk = lax.axis_index("group"), lax.axis_index("blk")
    dx, dy, dz, dcore = offset
    y = lax.rem(group // 2 + dy, 4)
    core = lax.rem(lax.rem(group, 2) + dcore, 2)
    x = lax.rem(blk // 4 + dx, 4)
    z = lax.rem(lax.rem(blk, 4) + dz, 4)
    return (y * 2 + core, x * 4 + z)


def row_of(offset):
    dx, dy, _, dcore = offset
    return (dx * 4 + dy) * 2 + dcore


def eye(size):
    rows = lax.broadcasted_iota(jnp.int32, (size, size), 0)
    return rows == lax.broadcasted_iota(jnp.int32, (size, size), 1)


def diagonals(matrix):
    size = matrix.shape[0]
    on = eye(LANES)
    columns, rows = [], []
    for i in range(0, size, LANES):
        block = jnp.where(on, matrix[i : i + LANES, i : i + LANES], 0.0)
        columns.append(jnp.sum(block, axis=1, keepdims=True))
        rows.append(jnp.sum(block, axis=0, keepdims=True))
    return jnp.concatenate(columns, 0), jnp.concatenate(rows, 1)


def parted(matrix):
    column, row = diagonals(matrix)
    off = jnp.where(eye(matrix.shape[0]), 0.0, matrix)
    return matrix, off, off.astype(BF16), column, row


def times(left, right):
    inner = jnp.dot(left[2], right[2], preferred_element_type=F32)
    return inner + left[3] * right[0] + left[1] * right[4]


def polynomial_chain(gram_ref, factor_ref, turn_ref):
    for step in range(ITERS):
        gram = parted(gram_ref[...])
        square = times(gram, gram)
        one = jnp.where(eye(square.shape[0]), linear_coefficient, 0.0)
        poly = parted(coef_b * gram[0] + coef_c * square + one)
        last = step == ITERS - 1
        if not last:
            turn_ref[...] = times(poly, gram)
        if step == 0:
            factor_ref[...] = poly[0]
        else:
            factor_ref[...] = times(poly, parted(factor_ref[...]))
        if not last:
            gram_ref[...] = times(poly, parted(turn_ref[...]))


def kernel(
    gradient,
    momentum,
    owners_ref,
    upd_v,
    mom_v,
    slot_ref,
    grad_v,
    tx,
    rx,
    tx2,
    rx2,
    norms,
    gram_ref,
    factor_ref,
    turn_ref,
    grad_sem,
    mom_sem,
    send_sem,
    recv_sem,
    send2_sem,
    recv2_sem,
    own_sem,
    norm_send,
    norm_recv,
):
    group, blk = lax.axis_index("group"), lax.axis_index("blk")
    me = group * 16 + blk
    core = lax.rem(group, 2)
    count, rows, width = grad_v.shape
    tiles = width // LANES
    full_rows = rows * count
    per = count // CHUNKS

    def load(c):
        part = pl.ds(c * per, per)
        return (
            pltpu.make_async_copy(gradient.at[part], grad_v.at[part], grad_sem.at[c]),
            pltpu.make_async_copy(momentum.at[part], mom_v.at[part], mom_sem.at[c]),
        )

    for c in range(CHUNKS):
        for copy in load(c):
            copy.start()

    barrier = pltpu.get_barrier_semaphore()

    def digits(k):
        return (k // 32, (k // 8) % 4, (k // 2) % 4, k % 2)

    for k in range(1, count):
        pl.semaphore_signal(barrier, inc=1, device_id=shifted(digits(k)), device_id_type=MESH)

    def ready(c):
        for copy in load(c):
            copy.wait()

        @pl.loop(0, per)
        def _(i):
            m = c * per + i
            for j in range(tiles):
                lanes = pl.ds(j * LANES, LANES)
                new = decay_rate * mom_v[m, :, lanes] + grad_v[m, :, lanes].astype(F32)
                mom_v[m, :, lanes] = new
                tx[m, j] = new.astype(BF16)

    for c in range(CHUNKS):
        ready(c)
    pl.semaphore_wait(barrier, count - 1)

    def send(offset, wave):
        device = shifted(offset)
        return pltpu.make_async_remote_copy(
            src_ref=tx.at[device[0] * 16 + device[1]],
            dst_ref=rx.at[:, me],
            send_sem=send_sem.at[wave],
            recv_sem=recv_sem.at[0],
            device_id=device,
            device_id_type=MESH,
        )

    own = pltpu.make_async_copy(tx.at[me], rx.at[:, me], own_sem.at[0])
    own.start()
    def sent(blocks, sem):
        part = tx.at[pl.ds(0, blocks)]
        return pltpu.make_async_remote_copy(
            src_ref=part,
            dst_ref=part,
            send_sem=sem,
            recv_sem=recv_sem.at[0],
            device_id=(group, blk),
            device_id_type=MESH,
        )

    for wave in range(2):
        for chip in CHIP_ORDER:
            send((*chip, lax.rem(core + wave, 2)), wave).start()
        if wave == 0:
            sent(count // 2 - 1, send_sem.at[0]).wait_send()
    send((0, 0, 0, 1), 1).start()

    own.wait()
    sent(count - 1, send_sem.at[1]).wait_recv()

    x_in = rx.reshape(tiles, full_rows, LANES)
    gram = None
    for j in range(0, tiles, 2):
        pair = jnp.concatenate([x_in[j], x_in[j + 1]], axis=1)
        term = lax.dot_general(pair, pair, (((1,), (1,)), ((), ())), preferred_element_type=F32)
        gram = term if gram is None else gram + term
    norm = jnp.sqrt(jnp.sum(diagonals(gram)[1]))
    norms[me] = jnp.full((1, LANES), norm, F32)

    def spread_blk(k):
        return pltpu.make_async_remote_copy(
            src_ref=norms.at[me],
            dst_ref=norms.at[me],
            send_sem=norm_send.at[0],
            recv_sem=norm_recv.at[0],
            device_id=(group, lax.rem(blk + k, 16)),
            device_id_type=MESH,
        )

    def spread_group(k):
        part = pl.ds(group * 16, 16)
        return pltpu.make_async_remote_copy(
            src_ref=norms.at[part],
            dst_ref=norms.at[part],
            send_sem=norm_send.at[1],
            recv_sem=norm_recv.at[1],
            device_id=(lax.rem(group + k, 8), blk),
            device_id_type=MESH,
        )

    def spread_all(blocks, at):
        part = norms.at[pl.ds(0, blocks)]
        return pltpu.make_async_remote_copy(
            src_ref=part,
            dst_ref=part,
            send_sem=norm_send.at[at],
            recv_sem=norm_recv.at[at],
            device_id=(group, blk),
            device_id_type=MESH,
        )

    for k in range(1, 16):
        spread_blk(k).start()

    inverse = 1.0 / (jnp.full((1, 1), norm, F32) + epsilon)
    gram_ref[...] = gram * (inverse * inverse)
    polynomial_chain(gram_ref, factor_ref, turn_ref)

    factor = parted(factor_ref[...])
    scale = 0.2 * math.sqrt(max(full_rows, width))
    x_out = tx2.reshape(tiles, full_rows, LANES)
    for j in range(0, tiles, 2):
        pair = jnp.concatenate([x_in[j], x_in[j + 1]], axis=1)
        mixed = jnp.dot(factor[2], pair, preferred_element_type=F32)
        final = ((mixed + factor[3] * pair.astype(F32)) * inverse).astype(BF16)
        scaled = (scale * final.astype(F32)).astype(BF16)
        x_out[j] = scaled[:, :LANES]
        x_out[j + 1] = scaled[:, LANES:]

    def back(offset):
        device = shifted(offset)
        return pltpu.make_async_remote_copy(
            src_ref=tx2.at[:, device[0] * 16 + device[1]],
            dst_ref=rx2.at[me],
            send_sem=send2_sem.at[0],
            recv_sem=recv2_sem.at[row_of(offset)],
            device_id=device,
            device_id_type=MESH,
        )

    own2 = pltpu.make_async_copy(tx2.at[:, me], rx2.at[me], own_sem.at[1])
    own2.start()
    for chip in CHIP_ORDER:
        for other_core in range(2):
            back((*chip, other_core)).start()
    back((0, 0, 0, 1)).start()

    spread_all(15, 0).wait()
    for k in range(1, 8):
        spread_group(k).start()

    def arrived(m):
        for j in range(tiles):
            upd_v[m, :, pl.ds(j * LANES, LANES)] = rx2[m, j]

    def row_arrived(dx, dy, dcore, steps):
        part = rx2.at[pl.ds(0, len(steps))]
        pltpu.make_async_remote_copy(
            src_ref=part,
            dst_ref=part,
            send_sem=send2_sem.at[0],
            recv_sem=recv2_sem.at[row_of((dx, dy, 0, dcore))],
            device_id=(group, blk),
            device_id_type=MESH,
        ).wait_recv()
        for dz in steps:
            gone = shifted((lax.rem(4 - dx, 4), lax.rem(4 - dy, 4), (4 - dz) % 4, dcore))
            arrived(gone[0] * 16 + gone[1])

    for wave in range(2):
        turn = lax.rem(core + wave, 2)

        @pl.loop(0, 15)
        def _(i):
            row_arrived((15 - i) // 4, lax.rem(15 - i, 4), turn, (2, 1, 3, 0))

        if wave == 0:
            own2.wait()
            arrived(me)

    row_arrived(0, 0, 0, (2, 1, 3))
    row_arrived(0, 0, 1, (2, 1, 3, 0))

    spread_all(7 * 16, 1).wait()

    other = jnp.broadcast_to(owners_ref[...], (count, LANES))
    owner = jnp.transpose(other.astype(F32)).astype(jnp.int32)
    row = lax.broadcasted_iota(jnp.int32, (count, LANES), 0)
    lane = lax.broadcasted_iota(jnp.int32, (count, LANES), 1)
    earlier = jnp.where((owner == other) & (lane < row), 1.0, 0.0)
    rank = jnp.sum(earlier, axis=1, keepdims=True).astype(jnp.int32)
    placing = owner * (SLOTS * 16) + rank
    spread = norms[:, 0, :] * (1.0 / math.sqrt(full_rows * width))
    chosen = jnp.where(placing == me * SLOTS + lane, spread, 0.0)
    slot_ref[...] = jnp.sum(chosen, axis=0, keepdims=True)[:, :SLOTS]

    sent(count // 2, send_sem.at[1]).wait_send()
    sent(count - 1, send2_sem.at[0]).wait_send()


def on_device(gradient, momentum, owner_group):
    count, rows, width = gradient.shape
    tiles = width // LANES
    full_rows = rows * count
    wide = (count, tiles, rows, LANES)
    tall = (tiles, count, rows, LANES)
    square = pltpu.VMEM((full_rows, full_rows), F32)
    dma = pltpu.SemaphoreType.DMA
    return pl.pallas_call(
        kernel,
        out_shape=(
            jax.ShapeDtypeStruct(gradient.shape, BF16),
            jax.ShapeDtypeStruct(momentum.shape, F32),
            jax.ShapeDtypeStruct((1, SLOTS), F32),
        ),
        in_specs=[
            pl.BlockSpec(memory_space=pl.ANY),
            pl.BlockSpec(memory_space=pl.ANY),
            pl.BlockSpec(memory_space=pltpu.VMEM),
        ],
        out_specs=(
            pl.BlockSpec(memory_space=pltpu.VMEM),
            pl.BlockSpec(memory_space=pltpu.VMEM),
            pl.BlockSpec(memory_space=pltpu.VMEM),
        ),
        scratch_shapes=[
            pltpu.VMEM(gradient.shape, BF16),
            pltpu.VMEM(wide, BF16),
            pltpu.VMEM(tall, BF16),
            pltpu.VMEM(tall, BF16),
            pltpu.VMEM(wide, BF16),
            pltpu.VMEM((count, 1, LANES), F32),
            square,
            square,
            square,
            dma((CHUNKS,)),
            dma((CHUNKS,)),
            dma((2,)),
            dma((1,)),
            dma((1,)),
            dma((32,)),
            dma((2,)),
            dma((2,)),
            dma((2,)),
        ],
        compiler_params=pltpu.CompilerParams(
            collective_id=0, has_side_effects=True, vmem_limit_bytes=44 << 20
        ),
    )(gradient, momentum, owner_group.reshape(1, count))


def solution(mesh):
    placed = (P(None, ("group", "blk"), None), P(None, ("group", "blk"), None), P())
    return jax.shard_map(
        on_device,
        mesh=mesh,
        in_specs=placed,
        out_specs=(
            P(None, ("group", "blk"), None),
            P(None, ("group", "blk"), None),
            P("group", "blk"),
        ),
        check_vma=False,
    )
```

```python
import functools
import math

import jax
import jax.numpy as jnp
from jax import lax
from jax.experimental import pallas as pl
from jax.experimental.pallas import tpu as pltpu
from jax.sharding import PartitionSpec as P

ITERS = 5
SLOTS = 2
linear_coefficient = 3.4445
coef_b = -4.775
coef_c = 2.0315
decay_rate = 0.95
epsilon = 1e-06

MESH = pl.DeviceIdType.MESH
F32 = jnp.float32
BF16 = jnp.bfloat16
LANES = 128
CHUNKS = 8


def hops(offset):
    return sum(min(step, 4 - step) for step in offset)


def chips_far_first():
    every = []
    for i in range(1, 64):
        a, b, c = i % 4, (i // 4) % 4, i // 16
        every.append((a, (a + b) % 4, (3 * a + c) % 4))
    return sorted(every, key=hops, reverse=True)


CHIP_ORDER = chips_far_first()
AHEAD = 63


def shifted(offset):
    group, blk = lax.axis_index("group"), lax.axis_index("blk")
    dx, dy, dz, dcore = offset
    y = lax.rem(group // 2 + dy, 4)
    core = lax.rem(lax.rem(group, 2) + dcore, 2)
    x = lax.rem(blk // 4 + dx, 4)
    z = lax.rem(lax.rem(blk, 4) + dz, 4)
    return (y * 2 + core, x * 4 + z)


def coordinate_tables():
    group, blk = lax.axis_index("group"), lax.axis_index("blk")
    doubled = [lax.rem(group // 2 + dy, 4) * 2 for dy in range(4)]
    along_x = [lax.rem(blk // 4 + dx, 4) * 4 for dx in range(4)]
    along_z = [lax.rem(lax.rem(blk, 4) + dz, 4) for dz in range(4)]
    groups = [[first + c for c in range(2)] for first in doubled]
    blks = [[first + second for second in along_z] for first in along_x]
    return groups, blks


def row_of(offset):
    dx, dy, _, dcore = offset
    return (dx * 4 + dy) * 2 + dcore


def eye(size):
    rows = lax.broadcasted_iota(jnp.int32, (size, size), 0)
    return rows == lax.broadcasted_iota(jnp.int32, (size, size), 1)


def diagonals(matrix):
    size = matrix.shape[0]
    on = eye(LANES)
    columns, rows = [], []
    for i in range(0, size, LANES):
        block = jnp.where(on, matrix[i : i + LANES, i : i + LANES], 0.0)
        columns.append(jnp.sum(block, axis=1, keepdims=True))
        rows.append(jnp.sum(block, axis=0, keepdims=True))
    return jnp.concatenate(columns, 0), jnp.concatenate(rows, 1)


def parted(matrix):
    column, row = diagonals(matrix)
    off = jnp.where(eye(matrix.shape[0]), 0.0, matrix)
    return matrix, off, off.astype(BF16), column, row


def times(left, right):
    inner = jnp.dot(left[2], right[2], preferred_element_type=F32)
    return inner + left[3] * right[0] + left[1] * right[4]


def polynomial_chain(gram_ref, factor_ref, turn_ref):
    for step in range(ITERS):
        gram = parted(gram_ref[...])
        square = times(gram, gram)
        one = jnp.where(eye(square.shape[0]), linear_coefficient, 0.0)
        poly = parted(coef_b * gram[0] + coef_c * square + one)
        last = step == ITERS - 1
        if not last:
            turn_ref[...] = times(poly, gram)
        if step == 0:
            factor_ref[...] = poly[0]
        else:
            factor_ref[...] = times(poly, parted(factor_ref[...]))
        if not last:
            gram_ref[...] = times(poly, parted(turn_ref[...]))


def kernel(
    gradient,
    momentum,
    owners,
    upd_v,
    mom_v,
    slot_ref,
    grad_v,
    owners_v,
    tx,
    rx,
    tx2,
    rx2,
    norms,
    gram_ref,
    factor_ref,
    turn_ref,
    grad_sem,
    mom_sem,
    send_sem,
    recv_sem,
    send2_sem,
    recv2_sem,
    own_sem,
    norm_send,
    norm_recv,
    mate_sem,
    chip_sem,
):
    group, blk = lax.axis_index("group"), lax.axis_index("blk")
    me = group * 16 + blk
    core = lax.rem(group, 2)
    groups, blks = coordinate_tables()
    count, rows, width = grad_v.shape
    tiles = width // LANES
    full_rows = rows * count
    per = count // CHUNKS

    def load(c):
        part = pl.ds(c * per, per)
        return (
            pltpu.make_async_copy(gradient.at[part], grad_v.at[part], grad_sem.at[c]),
            pltpu.make_async_copy(momentum.at[part], mom_v.at[part], mom_sem.at[c]),
        )

    for c in range(0, CHUNKS, 2):
        for copy in load(c):
            copy.start()

    owners_copy = pltpu.make_async_copy(owners, owners_v, own_sem.at[2])
    owners_copy.start()
    barrier = pltpu.get_barrier_semaphore()

    def digits(k):
        return (k // 32, (k // 8) % 4, (k // 2) % 4, k % 2)

    def device_at(chip, which):
        dx, dy, dz = chip
        return (groups[dy][which], blks[dx][dz])

    @pl.when(core == 0)
    def _():
        for chip in CHIP_ORDER:
            pl.semaphore_signal(
                barrier, inc=1, device_id=device_at(chip, 0), device_id_type=MESH
            )

    for c in range(1, CHUNKS, 2):
        for copy in load(c):
            copy.start()

    def ready(c):
        for copy in load(c):
            copy.wait()

        @pl.loop(0, per)
        def _(i):
            m = c * per + i
            for j in range(tiles):
                lanes = pl.ds(j * LANES, LANES)
                new = decay_rate * mom_v[m, :, lanes] + grad_v[m, :, lanes].astype(F32)
                mom_v[m, :, lanes] = new
                tx[m, j] = new.astype(BF16)

    for c in range(0, CHUNKS, 2):
        ready(c)
    mate = shifted((0, 0, 0, 1))

    @pl.when(core == 0)
    def _():
        pl.semaphore_wait(barrier, len(CHIP_ORDER))
        pl.semaphore_signal(barrier, inc=1, device_id=mate, device_id_type=MESH)

    @pl.when(core == 1)
    def _():
        pl.semaphore_wait(barrier, 1)
        pl.semaphore_signal(mate_sem, inc=1, device_id=mate, device_id_type=MESH)

    def send(device, send_sem):
        return pltpu.make_async_remote_copy(
            src_ref=tx.at[device[0] * 16 + device[1]],
            dst_ref=rx.at[:, me],
            send_sem=send_sem,
            recv_sem=recv_sem.at[0],
            device_id=device,
            device_id_type=MESH,
        )

    own = pltpu.make_async_copy(tx.at[me], rx.at[:, me], own_sem.at[0])

    def sent(blocks, sem):
        part = tx.at[pl.ds(0, blocks)]
        return pltpu.make_async_remote_copy(
            src_ref=part,
            dst_ref=part,
            send_sem=sem,
            recv_sem=recv_sem.at[0],
            device_id=(group, blk),
            device_id_type=MESH,
        )

    def all_in():
        @pl.when(core == 0)
        def _():
            pl.semaphore_wait(mate_sem, 1)
            for chip in CHIP_ORDER:
                pl.semaphore_signal(
                    chip_sem, inc=1, device_id=device_at(chip, 0), device_id_type=MESH
                )
            pl.semaphore_wait(chip_sem, len(CHIP_ORDER))
            pl.semaphore_signal(mate_sem, inc=1, device_id=mate, device_id_type=MESH)

        @pl.when(core == 1)
        def _():
            pl.semaphore_wait(mate_sem, 1)

    for i, chip in enumerate(CHIP_ORDER):
        send(device_at(chip, 0), send_sem.at[0 if i < AHEAD else 1]).start()

    @pl.when(core == 1)
    def _():
        send(mate, send_sem.at[2]).start()

    for c in range(1, CHUNKS, 2):
        ready(c)
    own.start()
    all_in()

    @pl.when(core == 0)
    def _():
        send(mate, send_sem.at[2]).start()

    sent(AHEAD, send_sem.at[0]).wait_send()
    for chip in CHIP_ORDER:
        send(device_at(chip, 1), send_sem.at[1]).start()

    own.wait()
    sent(count - 1, send_sem.at[1]).wait_recv()

    x_in = rx.reshape(tiles, full_rows, LANES)
    gram = None
    for j in range(0, tiles, 2):
        pair = jnp.concatenate([x_in[j], x_in[j + 1]], axis=1)
        term = lax.dot_general(pair, pair, (((1,), (1,)), ((), ())), preferred_element_type=F32)
        gram = term if gram is None else gram + term
    norm = jnp.sqrt(jnp.sum(diagonals(gram)[1]))
    norms[me] = jnp.full((1, LANES), norm, F32)

    def spread_blk(k):
        return pltpu.make_async_remote_copy(
            src_ref=norms.at[me],
            dst_ref=norms.at[me],
            send_sem=norm_send.at[0],
            recv_sem=norm_recv.at[0],
            device_id=(group, lax.rem(blk + k, 16)),
            device_id_type=MESH,
        )

    def spread_group(k):
        part = pl.ds(group * 16, 16)
        return pltpu.make_async_remote_copy(
            src_ref=norms.at[part],
            dst_ref=norms.at[part],
            send_sem=norm_send.at[1],
            recv_sem=norm_recv.at[1],
            device_id=(lax.rem(group + k, 8), blk),
            device_id_type=MESH,
        )

    def spread_all(blocks, at):
        part = norms.at[pl.ds(0, blocks)]
        return pltpu.make_async_remote_copy(
            src_ref=part,
            dst_ref=part,
            send_sem=norm_send.at[at],
            recv_sem=norm_recv.at[at],
            device_id=(group, blk),
            device_id_type=MESH,
        )

    for k in range(1, 16):
        spread_blk(k).start()

    inverse = 1.0 / (jnp.full((1, 1), norm, F32) + epsilon)
    gram_ref[...] = gram * (inverse * inverse)
    polynomial_chain(gram_ref, factor_ref, turn_ref)

    factor = parted(factor_ref[...])
    scale = 0.2 * math.sqrt(max(full_rows, width))
    x_out = tx2.reshape(tiles, full_rows, LANES)
    for j in range(0, tiles, 2):
        pair = jnp.concatenate([x_in[j], x_in[j + 1]], axis=1)
        mixed = jnp.dot(factor[2], pair, preferred_element_type=F32)
        final = ((mixed + factor[3] * pair.astype(F32)) * inverse).astype(BF16)
        scaled = (scale * final.astype(F32)).astype(BF16)
        x_out[j] = scaled[:, :LANES]
        x_out[j + 1] = scaled[:, LANES:]

    def back(offset):
        device = shifted(offset)
        return pltpu.make_async_remote_copy(
            src_ref=tx2.at[:, device[0] * 16 + device[1]],
            dst_ref=rx2.at[me],
            send_sem=send2_sem.at[0],
            recv_sem=recv2_sem.at[row_of(offset)],
            device_id=device,
            device_id_type=MESH,
        )

    own2 = pltpu.make_async_copy(tx2.at[:, me], rx2.at[me], own_sem.at[1])
    own2.start()
    for chip in CHIP_ORDER:
        for other_core in range(2):
            back((*chip, other_core)).start()
    back((0, 0, 0, 1)).start()

    spread_all(15, 0).wait()
    for k in range(1, 8):
        spread_group(k).start()

    def arrived(m):
        for j in range(tiles):
            upd_v[m, :, pl.ds(j * LANES, LANES)] = rx2[m, j]

    def row_arrived(dx, dy, dcore, steps):
        part = rx2.at[pl.ds(0, len(steps))]
        pltpu.make_async_remote_copy(
            src_ref=part,
            dst_ref=part,
            send_sem=send2_sem.at[0],
            recv_sem=recv2_sem.at[row_of((dx, dy, 0, dcore))],
            device_id=(group, blk),
            device_id_type=MESH,
        ).wait_recv()
        for dz in steps:
            gone = shifted((lax.rem(4 - dx, 4), lax.rem(4 - dy, 4), (4 - dz) % 4, dcore))
            arrived(gone[0] * 16 + gone[1])

    def fill_slots():
        spread_all(7 * 16, 1).wait()

        owners_copy.wait()
        other = jnp.broadcast_to(owners_v[...], (count, LANES))
        owner = jnp.transpose(other.astype(F32)).astype(jnp.int32)
        row = lax.broadcasted_iota(jnp.int32, (count, LANES), 0)
        lane = lax.broadcasted_iota(jnp.int32, (count, LANES), 1)
        earlier = jnp.where((owner == other) & (lane < row), 1.0, 0.0)
        rank = jnp.sum(earlier, axis=1, keepdims=True).astype(jnp.int32)
        placing = owner * (SLOTS * 16) + rank
        spread = norms[:, 0, :] * (1.0 / math.sqrt(full_rows * width))
        chosen = jnp.where(placing == me * SLOTS + lane, spread, 0.0)
        slot_ref[...] = jnp.sum(chosen, axis=0, keepdims=True)[:, :SLOTS]

    for wave in range(2):
        turn = lax.rem(core + wave, 2)

        @pl.loop(0, 15)
        def _(i):
            row_arrived((15 - i) // 4, lax.rem(15 - i, 4), turn, (2, 1, 3, 0))

        if wave == 0:
            own2.wait()
            arrived(me)
            fill_slots()

    row_arrived(0, 0, 0, (2, 1, 3))
    row_arrived(0, 0, 1, (2, 1, 3, 0))

    sent(count - 2 - AHEAD, send_sem.at[1]).wait_send()
    sent(1, send_sem.at[2]).wait_send()
    sent(count - 1, send2_sem.at[0]).wait_send()


def in_hbm(array):
    return pltpu.with_memory_space_constraint(array, pltpu.HBM)


def on_device(gradient, momentum, owner_group):
    count, rows, width = gradient.shape
    tiles = width // LANES
    full_rows = rows * count
    wide = (count, tiles, rows, LANES)
    tall = (tiles, count, rows, LANES)
    square = pltpu.VMEM((full_rows, full_rows), F32)
    dma = pltpu.SemaphoreType.DMA
    return pl.pallas_call(
        kernel,
        out_shape=(
            jax.ShapeDtypeStruct(gradient.shape, BF16),
            jax.ShapeDtypeStruct(momentum.shape, F32),
            jax.ShapeDtypeStruct((1, SLOTS), F32),
        ),
        in_specs=[
            pl.BlockSpec(memory_space=pl.ANY),
            pl.BlockSpec(memory_space=pl.ANY),
            pl.BlockSpec(memory_space=pl.ANY),
        ],
        out_specs=(
            pl.BlockSpec(memory_space=pltpu.VMEM),
            pl.BlockSpec(memory_space=pltpu.VMEM),
            pl.BlockSpec(memory_space=pltpu.VMEM),
        ),
        scratch_shapes=[
            pltpu.VMEM(gradient.shape, BF16),
            pltpu.VMEM((1, count), jnp.int32),
            pltpu.VMEM(wide, BF16),
            pltpu.VMEM(tall, BF16),
            pltpu.VMEM(tall, BF16),
            pltpu.VMEM(wide, BF16),
            pltpu.VMEM((count, 1, LANES), F32),
            square,
            square,
            square,
            dma((CHUNKS,)),
            dma((CHUNKS,)),
            dma((3,)),
            dma((1,)),
            dma((1,)),
            dma((32,)),
            dma((3,)),
            dma((2,)),
            dma((2,)),
            pltpu.SemaphoreType.REGULAR,
            pltpu.SemaphoreType.REGULAR,
        ],
        compiler_params=pltpu.CompilerParams(
            collective_id=0, has_side_effects=True, vmem_limit_bytes=44 << 20
        ),
    )(*(in_hbm(x) for x in (gradient, momentum, owner_group.reshape(1, count))))


def solution(mesh):
    placed = (P(None, ("group", "blk"), None), P(None, ("group", "blk"), None), P())
    return jax.shard_map(
        on_device,
        mesh=mesh,
        in_specs=placed,
        out_specs=(
            P(None, ("group", "blk"), None),
            P(None, ("group", "blk"), None),
            P("group", "blk"),
        ),
        check_vma=False,
    )
```

```python
import functools
import math

import jax
import jax.numpy as jnp
from jax import lax
from jax.experimental import pallas as pl
from jax.experimental.pallas import tpu as pltpu
from jax.sharding import PartitionSpec as P

ITERS = 5
SLOTS = 2
linear_coefficient = 3.4445
coef_b = -4.775
coef_c = 2.0315
decay_rate = 0.95
epsilon = 1e-06

MESH = pl.DeviceIdType.MESH
F32 = jnp.float32
BF16 = jnp.bfloat16
LANES = 128
CHUNKS = 8


def hops(offset):
    return sum(min(step, 4 - step) for step in offset)


def chips_far_first():
    every = []
    for i in range(1, 64):
        a, b, c = i % 4, (i // 4) % 4, i // 16
        every.append((a, (a + b) % 4, (3 * a + c) % 4))
    return sorted(every, key=hops, reverse=True)


CHIP_ORDER = chips_far_first()
AHEAD = 63


def shifted(offset):
    group, blk = lax.axis_index("group"), lax.axis_index("blk")
    dx, dy, dz, dcore = offset
    y = lax.rem(group // 2 + dy, 4)
    core = lax.rem(lax.rem(group, 2) + dcore, 2)
    x = lax.rem(blk // 4 + dx, 4)
    z = lax.rem(lax.rem(blk, 4) + dz, 4)
    return (y * 2 + core, x * 4 + z)


def coordinate_tables():
    group, blk = lax.axis_index("group"), lax.axis_index("blk")
    doubled = [lax.rem(group // 2 + dy, 4) * 2 for dy in range(4)]
    along_x = [lax.rem(blk // 4 + dx, 4) * 4 for dx in range(4)]
    along_z = [lax.rem(lax.rem(blk, 4) + dz, 4) for dz in range(4)]
    groups = [[first + c for c in range(2)] for first in doubled]
    blks = [[first + second for second in along_z] for first in along_x]
    return groups, blks


def eye(size):
    rows = lax.broadcasted_iota(jnp.int32, (size, size), 0)
    return rows == lax.broadcasted_iota(jnp.int32, (size, size), 1)


def diagonals(matrix):
    size = matrix.shape[0]
    on = eye(LANES)
    columns, rows = [], []
    for i in range(0, size, LANES):
        block = jnp.where(on, matrix[i : i + LANES, i : i + LANES], 0.0)
        columns.append(jnp.sum(block, axis=1, keepdims=True))
        rows.append(jnp.sum(block, axis=0, keepdims=True))
    return jnp.concatenate(columns, 0), jnp.concatenate(rows, 1)


def parted(matrix):
    column, row = diagonals(matrix)
    off = jnp.where(eye(matrix.shape[0]), 0.0, matrix)
    return matrix, off, off.astype(BF16), column, row


def times(left, right):
    inner = jnp.dot(left[2], right[2], preferred_element_type=F32)
    return inner + left[3] * right[0] + left[1] * right[4]


def polynomial_chain(gram_ref, factor_ref, turn_ref):
    for step in range(ITERS):
        gram = parted(gram_ref[...])
        square = times(gram, gram)
        one = jnp.where(eye(square.shape[0]), linear_coefficient, 0.0)
        poly = parted(coef_b * gram[0] + coef_c * square + one)
        last = step == ITERS - 1
        if not last:
            turn_ref[...] = times(poly, gram)
        if step == 0:
            factor_ref[...] = poly[0]
        else:
            factor_ref[...] = times(poly, parted(factor_ref[...]))
        if not last:
            gram_ref[...] = times(poly, parted(turn_ref[...]))


def kernel(
    gradient,
    momentum,
    owners,
    rx2,
    mom_v,
    slot_ref,
    grad_v,
    owners_v,
    tx,
    rx,
    tx2,
    norms,
    gram_ref,
    factor_ref,
    turn_ref,
    grad_sem,
    mom_sem,
    send_sem,
    recv_sem,
    send2_sem,
    recv2_sem,
    own_sem,
    norm_send,
    norm_recv,
    mate_sem,
    chip_sem,
):
    group, blk = lax.axis_index("group"), lax.axis_index("blk")
    me = group * 16 + blk
    core = lax.rem(group, 2)
    groups, blks = coordinate_tables()
    count, rows, width = grad_v.shape
    tiles = width // LANES
    full_rows = rows * count
    per = count // CHUNKS

    def load(c):
        part = pl.ds(c * per, per)
        return (
            pltpu.make_async_copy(gradient.at[part], grad_v.at[part], grad_sem.at[c]),
            pltpu.make_async_copy(momentum.at[part], mom_v.at[part], mom_sem.at[c]),
        )

    for c in range(0, CHUNKS, 2):
        for copy in load(c):
            copy.start()

    owners_copy = pltpu.make_async_copy(owners, owners_v, own_sem.at[2])
    owners_copy.start()
    barrier = pltpu.get_barrier_semaphore()

    def digits(k):
        return (k // 32, (k // 8) % 4, (k // 2) % 4, k % 2)

    def device_at(chip, which):
        dx, dy, dz = chip
        return (groups[dy][which], blks[dx][dz])

    @pl.when(core == 0)
    def _():
        for chip in CHIP_ORDER:
            pl.semaphore_signal(
                barrier, inc=1, device_id=device_at(chip, 0), device_id_type=MESH
            )

    for c in range(1, CHUNKS, 2):
        for copy in load(c):
            copy.start()

    def ready(c):
        for copy in load(c):
            copy.wait()

        @pl.loop(0, per)
        def _(i):
            m = c * per + i
            for j in range(tiles):
                lanes = pl.ds(j * LANES, LANES)
                new = decay_rate * mom_v[m, :, lanes] + grad_v[m, :, lanes].astype(F32)
                mom_v[m, :, lanes] = new
                tx[m, j] = new.astype(BF16)

    for c in range(0, CHUNKS, 2):
        ready(c)
    mate = shifted((0, 0, 0, 1))

    @pl.when(core == 0)
    def _():
        pl.semaphore_wait(barrier, len(CHIP_ORDER))
        pl.semaphore_signal(barrier, inc=1, device_id=mate, device_id_type=MESH)

    @pl.when(core == 1)
    def _():
        pl.semaphore_wait(barrier, 1)
        pl.semaphore_signal(mate_sem, inc=1, device_id=mate, device_id_type=MESH)

    def send(device, send_sem):
        return pltpu.make_async_remote_copy(
            src_ref=tx.at[device[0] * 16 + device[1]],
            dst_ref=rx.at[:, me],
            send_sem=send_sem,
            recv_sem=recv_sem.at[0],
            device_id=device,
            device_id_type=MESH,
        )

    own = pltpu.make_async_copy(tx.at[me], rx.at[:, me], own_sem.at[0])

    def sent(blocks, sem):
        part = tx.at[pl.ds(0, blocks)]
        return pltpu.make_async_remote_copy(
            src_ref=part,
            dst_ref=part,
            send_sem=sem,
            recv_sem=recv_sem.at[0],
            device_id=(group, blk),
            device_id_type=MESH,
        )

    def all_in():
        @pl.when(core == 0)
        def _():
            pl.semaphore_wait(mate_sem, 1)
            for chip in CHIP_ORDER:
                pl.semaphore_signal(
                    chip_sem, inc=1, device_id=device_at(chip, 0), device_id_type=MESH
                )
            pl.semaphore_wait(chip_sem, len(CHIP_ORDER))
            pl.semaphore_signal(mate_sem, inc=1, device_id=mate, device_id_type=MESH)

        @pl.when(core == 1)
        def _():
            pl.semaphore_wait(mate_sem, 1)

    for i, chip in enumerate(CHIP_ORDER):
        send(device_at(chip, 0), send_sem.at[0 if i < AHEAD else 1]).start()

    @pl.when(core == 1)
    def _():
        send(mate, send_sem.at[2]).start()

    for c in range(1, CHUNKS, 2):
        ready(c)
    own.start()
    all_in()

    @pl.when(core == 0)
    def _():
        send(mate, send_sem.at[2]).start()

    sent(AHEAD, send_sem.at[0]).wait_send()
    for chip in CHIP_ORDER:
        send(device_at(chip, 1), send_sem.at[1]).start()

    own.wait()
    sent(count - 1, send_sem.at[1]).wait_recv()

    x_in = rx.reshape(tiles, full_rows, LANES)
    gram = None
    for j in range(0, tiles, 2):
        pair = jnp.concatenate([x_in[j], x_in[j + 1]], axis=1)
        term = lax.dot_general(pair, pair, (((1,), (1,)), ((), ())), preferred_element_type=F32)
        gram = term if gram is None else gram + term
    norm = jnp.sqrt(jnp.sum(diagonals(gram)[1]))
    norms[me] = jnp.full((1, LANES), norm, F32)

    def spread_blk(k):
        return pltpu.make_async_remote_copy(
            src_ref=norms.at[me],
            dst_ref=norms.at[me],
            send_sem=norm_send.at[0],
            recv_sem=norm_recv.at[0],
            device_id=(group, lax.rem(blk + k, 16)),
            device_id_type=MESH,
        )

    def spread_group(k):
        part = pl.ds(group * 16, 16)
        return pltpu.make_async_remote_copy(
            src_ref=norms.at[part],
            dst_ref=norms.at[part],
            send_sem=norm_send.at[1],
            recv_sem=norm_recv.at[1],
            device_id=(lax.rem(group + k, 8), blk),
            device_id_type=MESH,
        )

    def spread_all(blocks, at):
        part = norms.at[pl.ds(0, blocks)]
        return pltpu.make_async_remote_copy(
            src_ref=part,
            dst_ref=part,
            send_sem=norm_send.at[at],
            recv_sem=norm_recv.at[at],
            device_id=(group, blk),
            device_id_type=MESH,
        )

    for k in range(1, 16):
        spread_blk(k).start()

    inverse = 1.0 / (jnp.full((1, 1), norm, F32) + epsilon)
    gram_ref[...] = gram * (inverse * inverse)
    polynomial_chain(gram_ref, factor_ref, turn_ref)

    factor = parted(factor_ref[...])
    scale = 0.2 * math.sqrt(max(full_rows, width))
    x_out = tx2.reshape(tiles, full_rows, LANES)
    for j in range(0, tiles, 2):
        pair = jnp.concatenate([x_in[j], x_in[j + 1]], axis=1)
        mixed = jnp.dot(factor[2], pair, preferred_element_type=F32)
        final = ((mixed + factor[3] * pair.astype(F32)) * inverse).astype(BF16)
        scaled = (scale * final.astype(F32)).astype(BF16)
        x_out[j] = scaled[:, :LANES]
        x_out[j + 1] = scaled[:, LANES:]

    def back(offset):
        device = shifted(offset)
        return pltpu.make_async_remote_copy(
            src_ref=tx2.at[:, device[0] * 16 + device[1]],
            dst_ref=rx2.at[me],
            send_sem=send2_sem.at[0],
            recv_sem=recv2_sem.at[0],
            device_id=device,
            device_id_type=MESH,
        )

    own2 = pltpu.make_async_copy(tx2.at[:, me], rx2.at[me], own_sem.at[1])
    own2.start()
    for chip in CHIP_ORDER:
        for other_core in range(2):
            back((*chip, other_core)).start()
    back((0, 0, 0, 1)).start()

    spread_all(15, 0).wait()
    for k in range(1, 8):
        spread_group(k).start()

    def fill_slots():
        spread_all(7 * 16, 1).wait()

        owners_copy.wait()
        other = jnp.broadcast_to(owners_v[...], (count, LANES))
        owner = jnp.transpose(other.astype(F32)).astype(jnp.int32)
        row = lax.broadcasted_iota(jnp.int32, (count, LANES), 0)
        lane = lax.broadcasted_iota(jnp.int32, (count, LANES), 1)
        earlier = jnp.where((owner == other) & (lane < row), 1.0, 0.0)
        rank = jnp.sum(earlier, axis=1, keepdims=True).astype(jnp.int32)
        placing = owner * (SLOTS * 16) + rank
        spread = norms[:, 0, :] * (1.0 / math.sqrt(full_rows * width))
        chosen = jnp.where(placing == me * SLOTS + lane, spread, 0.0)
        slot_ref[...] = jnp.sum(chosen, axis=0, keepdims=True)[:, :SLOTS]

    fill_slots()
    own2.wait()
    part = rx2.at[pl.ds(0, count - 1)]
    pltpu.make_async_remote_copy(
        src_ref=part,
        dst_ref=part,
        send_sem=send2_sem.at[0],
        recv_sem=recv2_sem.at[0],
        device_id=(group, blk),
        device_id_type=MESH,
    ).wait_recv()

    sent(count - 2 - AHEAD, send_sem.at[1]).wait_send()
    sent(1, send_sem.at[2]).wait_send()
    sent(count - 1, send2_sem.at[0]).wait_send()


def in_hbm(array):
    return pltpu.with_memory_space_constraint(array, pltpu.HBM)


def store_all(update, momentum_out, slots, update_hbm, momentum_hbm, slots_hbm, sems):
    tiles = update.shape[1]
    copies = [
        pltpu.make_async_copy(slots, slots_hbm, sems.at[0]),
        pltpu.make_async_copy(momentum_out, momentum_hbm, sems.at[1]),
    ]
    for j in range(tiles):
        lanes = pl.ds(j * LANES, LANES)
        copies.append(
            pltpu.make_async_copy(update.at[:, j], update_hbm.at[:, :, lanes], sems.at[2 + j])
        )
    for copy in copies:
        copy.start()
    for copy in copies:
        copy.wait()


def on_device(gradient, momentum, owner_group):
    count, rows, width = gradient.shape
    tiles = width // LANES
    full_rows = rows * count
    wide = (count, tiles, rows, LANES)
    tall = (tiles, count, rows, LANES)
    square = pltpu.VMEM((full_rows, full_rows), F32)
    dma = pltpu.SemaphoreType.DMA
    results = pl.pallas_call(
        kernel,
        out_shape=(
            jax.ShapeDtypeStruct(wide, BF16),
            jax.ShapeDtypeStruct(momentum.shape, F32),
            jax.ShapeDtypeStruct((1, SLOTS), F32),
        ),
        in_specs=[
            pl.BlockSpec(memory_space=pl.ANY),
            pl.BlockSpec(memory_space=pl.ANY),
            pl.BlockSpec(memory_space=pl.ANY),
        ],
        out_specs=(
            pl.BlockSpec(memory_space=pltpu.VMEM),
            pl.BlockSpec(memory_space=pltpu.VMEM),
            pl.BlockSpec(memory_space=pltpu.VMEM),
        ),
        scratch_shapes=[
            pltpu.VMEM(gradient.shape, BF16),
            pltpu.VMEM((1, count), jnp.int32),
            pltpu.VMEM(wide, BF16),
            pltpu.VMEM(tall, BF16),
            pltpu.VMEM(tall, BF16),
            pltpu.VMEM((count, 1, LANES), F32),
            square,
            square,
            square,
            dma((CHUNKS,)),
            dma((CHUNKS,)),
            dma((3,)),
            dma((1,)),
            dma((1,)),
            dma((1,)),
            dma((3,)),
            dma((2,)),
            dma((2,)),
            pltpu.SemaphoreType.REGULAR,
            pltpu.SemaphoreType.REGULAR,
        ],
        compiler_params=pltpu.CompilerParams(
            collective_id=0, has_side_effects=True, vmem_limit_bytes=44 << 20
        ),
    )(*(in_hbm(x) for x in (gradient, momentum, owner_group.reshape(1, count))))
    return pl.pallas_call(
        store_all,
        out_shape=(
            jax.ShapeDtypeStruct(gradient.shape, BF16),
            jax.ShapeDtypeStruct(momentum.shape, F32),
            jax.ShapeDtypeStruct((1, SLOTS), F32),
        ),
        in_specs=[pl.BlockSpec(memory_space=pl.ANY)] * 3,
        out_specs=(pl.BlockSpec(memory_space=pl.ANY),) * 3,
        scratch_shapes=[dma((2 + tiles,))],
        compiler_params=pltpu.CompilerParams(vmem_limit_bytes=1 << 20),
    )(*results)


def solution(mesh):
    placed = (P(None, ("group", "blk"), None), P(None, ("group", "blk"), None), P())
    return jax.shard_map(
        on_device,
        mesh=mesh,
        in_specs=placed,
        out_specs=(
            P(None, ("group", "blk"), None),
            P(None, ("group", "blk"), None),
            P("group", "blk"),
        ),
        check_vma=False,
    )
```

```python
import functools
import math

import jax
import jax.numpy as jnp
from jax import lax
from jax.experimental import pallas as pl
from jax.experimental.pallas import tpu as pltpu
from jax.sharding import PartitionSpec as P

ITERS = 5
SLOTS = 2
linear_coefficient = 3.4445
coef_b = -4.775
coef_c = 2.0315
decay_rate = 0.95
epsilon = 1e-06

MESH = pl.DeviceIdType.MESH
F32 = jnp.float32
BF16 = jnp.bfloat16
LANES = 128
CHUNKS = 8


def hops(offset):
    return sum(min(step, 4 - step) for step in offset)


def chips_far_first():
    every = []
    for i in range(1, 64):
        a, b, c = i % 4, (i // 4) % 4, i // 16
        every.append((a, (a + b) % 4, (3 * a + c) % 4))
    return sorted(every, key=hops, reverse=True)


CHIP_ORDER = chips_far_first()
AHEAD = 63


def shifted(offset):
    group, blk = lax.axis_index("group"), lax.axis_index("blk")
    dx, dy, dz, dcore = offset
    y = lax.rem(group // 2 + dy, 4)
    core = lax.rem(lax.rem(group, 2) + dcore, 2)
    x = lax.rem(blk // 4 + dx, 4)
    z = lax.rem(lax.rem(blk, 4) + dz, 4)
    return (y * 2 + core, x * 4 + z)


def coordinate_tables():
    group, blk = lax.axis_index("group"), lax.axis_index("blk")
    doubled = [lax.rem(group // 2 + dy, 4) * 2 for dy in range(4)]
    along_x = [lax.rem(blk // 4 + dx, 4) * 4 for dx in range(4)]
    along_z = [lax.rem(lax.rem(blk, 4) + dz, 4) for dz in range(4)]
    groups = [[first + c for c in range(2)] for first in doubled]
    blks = [[first + second for second in along_z] for first in along_x]
    return groups, blks


def eye(size):
    rows = lax.broadcasted_iota(jnp.int32, (size, size), 0)
    return rows == lax.broadcasted_iota(jnp.int32, (size, size), 1)


def diagonals(matrix):
    size = matrix.shape[0]
    on = eye(LANES)
    columns, rows = [], []
    for i in range(0, size, LANES):
        block = jnp.where(on, matrix[i : i + LANES, i : i + LANES], 0.0)
        columns.append(jnp.sum(block, axis=1, keepdims=True))
        rows.append(jnp.sum(block, axis=0, keepdims=True))
    return jnp.concatenate(columns, 0), jnp.concatenate(rows, 1)


def parted(matrix):
    column, row = diagonals(matrix)
    off = jnp.where(eye(matrix.shape[0]), 0.0, matrix)
    return matrix, off, off.astype(BF16), column, row


def times(left, right):
    inner = jnp.dot(left[2], right[2], preferred_element_type=F32)
    return inner + left[3] * right[0] + left[1] * right[4]


def polynomial_chain(gram_ref, factor_ref, turn_ref):
    for step in range(ITERS):
        gram = parted(gram_ref[...])
        square = times(gram, gram)
        one = jnp.where(eye(square.shape[0]), linear_coefficient, 0.0)
        poly = parted(coef_b * gram[0] + coef_c * square + one)
        last = step == ITERS - 1
        if not last:
            turn_ref[...] = times(poly, gram)
        if step == 0:
            factor_ref[...] = poly[0]
        else:
            factor_ref[...] = times(poly, parted(factor_ref[...]))
        if not last:
            gram_ref[...] = times(poly, parted(turn_ref[...]))


def kernel(
    gradient,
    momentum,
    owners,
    rx2,
    mom_v,
    slot_ref,
    grad_v,
    owners_v,
    tx,
    rx,
    tx2,
    norms,
    packed,
    gram_ref,
    factor_ref,
    turn_ref,
    grad_sem,
    mom_sem,
    send_sem,
    recv_sem,
    send2_sem,
    recv2_sem,
    own_sem,
    norm_send,
    norm_recv,
    mate_sem,
    chip_sem,
):
    group, blk = lax.axis_index("group"), lax.axis_index("blk")
    me = group * 16 + blk
    core = lax.rem(group, 2)
    groups, blks = coordinate_tables()
    count, rows, width = grad_v.shape
    tiles = width // LANES
    full_rows = rows * count
    per = count // CHUNKS

    def load(c):
        part = pl.ds(c * per, per)
        return (
            pltpu.make_async_copy(gradient.at[part], grad_v.at[part], grad_sem.at[c]),
            pltpu.make_async_copy(momentum.at[part], mom_v.at[part], mom_sem.at[c]),
        )

    for c in range(0, CHUNKS, 2):
        for copy in load(c):
            copy.start()

    owners_copy = pltpu.make_async_copy(owners, owners_v, own_sem.at[2])
    owners_copy.start()
    barrier = pltpu.get_barrier_semaphore()

    def digits(k):
        return (k // 32, (k // 8) % 4, (k // 2) % 4, k % 2)

    def device_at(chip, which):
        dx, dy, dz = chip
        return (groups[dy][which], blks[dx][dz])

    @pl.when(core == 0)
    def _():
        for chip in CHIP_ORDER:
            pl.semaphore_signal(
                barrier, inc=1, device_id=device_at(chip, 0), device_id_type=MESH
            )

    for c in range(1, CHUNKS, 2):
        for copy in load(c):
            copy.start()

    def ready(c):
        for copy in load(c):
            copy.wait()

        @pl.loop(0, per)
        def _(i):
            m = c * per + i
            for j in range(tiles):
                lanes = pl.ds(j * LANES, LANES)
                new = decay_rate * mom_v[m, :, lanes] + grad_v[m, :, lanes].astype(F32)
                mom_v[m, :, lanes] = new
                tx[m, j] = new.astype(BF16)

    for c in range(0, CHUNKS, 2):
        ready(c)
    mate = shifted((0, 0, 0, 1))

    @pl.when(core == 0)
    def _():
        pl.semaphore_wait(barrier, len(CHIP_ORDER))
        pl.semaphore_signal(barrier, inc=1, device_id=mate, device_id_type=MESH)

    @pl.when(core == 1)
    def _():
        pl.semaphore_wait(barrier, 1)
        pl.semaphore_signal(mate_sem, inc=1, device_id=mate, device_id_type=MESH)

    def send(device, send_sem):
        return pltpu.make_async_remote_copy(
            src_ref=tx.at[device[0] * 16 + device[1]],
            dst_ref=rx.at[:, me],
            send_sem=send_sem,
            recv_sem=recv_sem.at[0],
            device_id=device,
            device_id_type=MESH,
        )

    own = pltpu.make_async_copy(tx.at[me], rx.at[:, me], own_sem.at[0])

    def sent(blocks, sem):
        part = tx.at[pl.ds(0, blocks)]
        return pltpu.make_async_remote_copy(
            src_ref=part,
            dst_ref=part,
            send_sem=sem,
            recv_sem=recv_sem.at[0],
            device_id=(group, blk),
            device_id_type=MESH,
        )

    def all_in():
        @pl.when(core == 0)
        def _():
            pl.semaphore_wait(mate_sem, 1)
            for chip in CHIP_ORDER:
                pl.semaphore_signal(
                    chip_sem, inc=1, device_id=device_at(chip, 0), device_id_type=MESH
                )
            pl.semaphore_wait(chip_sem, len(CHIP_ORDER))
            pl.semaphore_signal(mate_sem, inc=1, device_id=mate, device_id_type=MESH)

        @pl.when(core == 1)
        def _():
            pl.semaphore_wait(mate_sem, 1)

    for i, chip in enumerate(CHIP_ORDER):
        send(device_at(chip, 0), send_sem.at[0 if i < AHEAD else 1]).start()

    @pl.when(core == 1)
    def _():
        send(mate, send_sem.at[2]).start()

    for c in range(1, CHUNKS, 2):
        ready(c)
    own.start()
    all_in()

    @pl.when(core == 0)
    def _():
        send(mate, send_sem.at[2]).start()

    sent(AHEAD, send_sem.at[0]).wait_send()
    for chip in CHIP_ORDER:
        send(device_at(chip, 1), send_sem.at[1]).start()

    own.wait()
    sent(count - 1, send_sem.at[1]).wait_recv()

    x_in = rx.reshape(tiles, full_rows, LANES)
    gram = None
    for j in range(0, tiles, 2):
        pair = jnp.concatenate([x_in[j], x_in[j + 1]], axis=1)
        term = lax.dot_general(pair, pair, (((1,), (1,)), ((), ())), preferred_element_type=F32)
        gram = term if gram is None else gram + term
    norm = jnp.sqrt(jnp.sum(diagonals(gram)[1]))
    norms[me] = jnp.full((1, LANES), norm, F32)

    def spread_blk(k):
        return pltpu.make_async_remote_copy(
            src_ref=norms.at[me],
            dst_ref=norms.at[me],
            send_sem=norm_send.at[0],
            recv_sem=norm_recv.at[0],
            device_id=(group, lax.rem(blk + k, 16)),
            device_id_type=MESH,
        )

    def spread_group(k):
        return pltpu.make_async_remote_copy(
            src_ref=packed.at[group],
            dst_ref=packed.at[group],
            send_sem=norm_send.at[1],
            recv_sem=norm_recv.at[1],
            device_id=(lax.rem(group + k, 8), blk),
            device_id_type=MESH,
        )

    def spread_all(ref, blocks, at):
        part = ref.at[pl.ds(0, blocks)]
        return pltpu.make_async_remote_copy(
            src_ref=part,
            dst_ref=part,
            send_sem=norm_send.at[at],
            recv_sem=norm_recv.at[at],
            device_id=(group, blk),
            device_id_type=MESH,
        )

    for k in range(1, 16):
        spread_blk(k).start()

    inverse = 1.0 / (jnp.full((1, 1), norm, F32) + epsilon)
    gram_ref[...] = gram * (inverse * inverse)
    polynomial_chain(gram_ref, factor_ref, turn_ref)

    factor = parted(factor_ref[...])
    scale = 0.2 * math.sqrt(max(full_rows, width))
    x_out = tx2.reshape(tiles, full_rows, LANES)
    for j in range(0, tiles, 2):
        pair = jnp.concatenate([x_in[j], x_in[j + 1]], axis=1)
        mixed = jnp.dot(factor[2], pair, preferred_element_type=F32)
        final = ((mixed + factor[3] * pair.astype(F32)) * inverse).astype(BF16)
        scaled = (scale * final.astype(F32)).astype(BF16)
        x_out[j] = scaled[:, :LANES]
        x_out[j + 1] = scaled[:, LANES:]

    def back(offset):
        device = shifted(offset)
        return pltpu.make_async_remote_copy(
            src_ref=tx2.at[:, device[0] * 16 + device[1]],
            dst_ref=rx2.at[me],
            send_sem=send2_sem.at[0],
            recv_sem=recv2_sem.at[0],
            device_id=device,
            device_id_type=MESH,
        )

    own2 = pltpu.make_async_copy(tx2.at[:, me], rx2.at[me], own_sem.at[1])
    own2.start()
    for chip in CHIP_ORDER:
        for other_core in range(2):
            back((*chip, other_core)).start()
    back((0, 0, 0, 1)).start()

    spread_all(norms, 15, 0).wait()
    sixteen = norms[pl.ds(group * 16, 16), 0, :]
    at_row = lax.broadcasted_iota(jnp.int32, (16, LANES), 0)
    at_lane = lax.broadcasted_iota(jnp.int32, (16, LANES), 1)
    packed[group] = jnp.sum(jnp.where(at_row == at_lane, sixteen, 0.0), axis=0, keepdims=True)
    for k in range(1, 8):
        spread_group(k).start()

    def fill_slots():
        spread_all(packed, 7, 1).wait()

        owners_copy.wait()
        other = jnp.broadcast_to(owners_v[...], (count, LANES))
        owner = jnp.transpose(other.astype(F32)).astype(jnp.int32)
        row = lax.broadcasted_iota(jnp.int32, (count, LANES), 0)
        lane = lax.broadcasted_iota(jnp.int32, (count, LANES), 1)
        earlier = jnp.where((owner == other) & (lane < row), 1.0, 0.0)
        rank = jnp.sum(earlier, axis=1, keepdims=True).astype(jnp.int32)
        placing = owner * (SLOTS * 16) + rank
        chosen_norm = jnp.broadcast_to(
            jnp.transpose(jnp.concatenate([packed[g][:, :16] for g in range(8)], axis=1)),
            (count, LANES),
        )
        spread = chosen_norm * (1.0 / math.sqrt(full_rows * width))
        chosen = jnp.where(placing == me * SLOTS + lane, spread, 0.0)
        slot_ref[...] = jnp.sum(chosen, axis=0, keepdims=True)[:, :SLOTS]

    fill_slots()
    own2.wait()
    part = rx2.at[pl.ds(0, count - 1)]
    pltpu.make_async_remote_copy(
        src_ref=part,
        dst_ref=part,
        send_sem=send2_sem.at[0],
        recv_sem=recv2_sem.at[0],
        device_id=(group, blk),
        device_id_type=MESH,
    ).wait_recv()

    sent(count - 2 - AHEAD, send_sem.at[1]).wait_send()
    sent(1, send_sem.at[2]).wait_send()
    sent(count - 1, send2_sem.at[0]).wait_send()


def in_hbm(array):
    return pltpu.with_memory_space_constraint(array, pltpu.HBM)


def store_all(update, momentum_out, slots, update_hbm, momentum_hbm, slots_hbm, sems):
    tiles = update.shape[1]
    copies = [
        pltpu.make_async_copy(slots, slots_hbm, sems.at[0]),
        pltpu.make_async_copy(momentum_out, momentum_hbm, sems.at[1]),
    ]
    for j in range(tiles):
        lanes = pl.ds(j * LANES, LANES)
        copies.append(
            pltpu.make_async_copy(update.at[:, j], update_hbm.at[:, :, lanes], sems.at[2 + j])
        )
    for copy in copies:
        copy.start()
    for copy in copies:
        copy.wait()


def on_device(gradient, momentum, owner_group):
    count, rows, width = gradient.shape
    tiles = width // LANES
    full_rows = rows * count
    wide = (count, tiles, rows, LANES)
    tall = (tiles, count, rows, LANES)
    square = pltpu.VMEM((full_rows, full_rows), F32)
    dma = pltpu.SemaphoreType.DMA
    results = pl.pallas_call(
        kernel,
        out_shape=(
            jax.ShapeDtypeStruct(wide, BF16),
            jax.ShapeDtypeStruct(momentum.shape, F32),
            jax.ShapeDtypeStruct((1, SLOTS), F32),
        ),
        in_specs=[
            pl.BlockSpec(memory_space=pl.ANY),
            pl.BlockSpec(memory_space=pl.ANY),
            pl.BlockSpec(memory_space=pl.ANY),
        ],
        out_specs=(
            pl.BlockSpec(memory_space=pltpu.VMEM),
            pl.BlockSpec(memory_space=pltpu.VMEM),
            pl.BlockSpec(memory_space=pltpu.VMEM),
        ),
        scratch_shapes=[
            pltpu.VMEM(gradient.shape, BF16),
            pltpu.VMEM((1, count), jnp.int32),
            pltpu.VMEM(wide, BF16),
            pltpu.VMEM(tall, BF16),
            pltpu.VMEM(tall, BF16),
            pltpu.VMEM((count, 1, LANES), F32),
            pltpu.VMEM((8, 1, LANES), F32),
            square,
            square,
            square,
            dma((CHUNKS,)),
            dma((CHUNKS,)),
            dma((3,)),
            dma((1,)),
            dma((1,)),
            dma((1,)),
            dma((3,)),
            dma((2,)),
            dma((2,)),
            pltpu.SemaphoreType.REGULAR,
            pltpu.SemaphoreType.REGULAR,
        ],
        compiler_params=pltpu.CompilerParams(
            collective_id=0, has_side_effects=True, vmem_limit_bytes=44 << 20
        ),
    )(*(in_hbm(x) for x in (gradient, momentum, owner_group.reshape(1, count))))
    return pl.pallas_call(
        store_all,
        out_shape=(
            jax.ShapeDtypeStruct(gradient.shape, BF16),
            jax.ShapeDtypeStruct(momentum.shape, F32),
            jax.ShapeDtypeStruct((1, SLOTS), F32),
        ),
        in_specs=[pl.BlockSpec(memory_space=pl.ANY)] * 3,
        out_specs=(pl.BlockSpec(memory_space=pl.ANY),) * 3,
        scratch_shapes=[dma((2 + tiles,))],
        compiler_params=pltpu.CompilerParams(vmem_limit_bytes=1 << 20),
    )(*results)


def solution(mesh):
    placed = (P(None, ("group", "blk"), None), P(None, ("group", "blk"), None), P())
    return jax.shard_map(
        on_device,
        mesh=mesh,
        in_specs=placed,
        out_specs=(
            P(None, ("group", "blk"), None),
            P(None, ("group", "blk"), None),
            P("group", "blk"),
        ),
        check_vma=False,
    )
```
